1024 devices in a mesh: dp: 64 (over x, z_hi, core), tensor: 16 (over y, z_lo).
Axes of the slice: x: 8, y: 8, z: 8 (z_hi: 4, z_lo: 2; z = z_hi * 2 + z_lo), core: 2. Of those that a mesh axis runs over, the one named last changes fastest.
Arguments:
- inputs: bfloat16 [16384, 4096], P('dp', 'tensor'), may hold values from -6 to 6
- first_factor: bfloat16 [256, 16, 1024], P(None, 'tensor'), may hold values from -0.375 to 0.375
- second_factor: bfloat16 [1024, 16, 1024], P(None, 'tensor'), may hold values from -0.1875 to 0.1875
- cotangent: bfloat16 [16384, 16384], P('tensor', 'dp'), may hold values from -6 to 6
Outputs:
- input_grad: bfloat16 [16384, 4096], P('dp', 'tensor')
- first_grad: float32 [256, 16, 1024], P('dp', 'tensor')
The draws below stay inside these ranges and needn't reach their ends.
All inputs are finite; a program needn't handle non-finite values.
Results may differ from the reference program's by a relative error of at most 0.0063.
Values may be sent and summed in bfloat16 or wider, within the bound.
A program may use at most 32 MiB of HBM per device.

```python
import jax
import jax.numpy as jnp
from jax import lax

MODEL_WIDTH = 4096
HIDDEN_SIZE = 16384
BLOCKS = 16
TOK_DEV = 256
TOKENS = 16384
IN_BLK = 256
OUT_BLK = 1024
GROUP = 64
N_DP = 64


def block_scale(key, dims, shards, least, high):
    gain, own = 1.0, jax.random.fold_in(key, 6)
    for dim, parts in shards:
        steps = jnp.exp(jax.random.uniform(jax.random.fold_in(own, dim), (parts,), jnp.float32, least / len(shards), high / len(shards)))
        gain = gain * jnp.repeat(steps, dims[dim] // parts).reshape([-1 if axis == dim else 1 for axis in range(len(dims))])
    return gain


def gaussian(key, shape, width, limit, split=(), held_as=jnp.bfloat16):
    drawn = width * jax.random.normal(key, shape, jnp.float32)
    if split:
        drawn = drawn * block_scale(key, shape, split, -0.22, 0.18)
    return jnp.clip(drawn, -limit, limit).astype(held_as)


def setup_inputs(seed: int = 0) -> dict:
    key_list = jax.random.split(jax.random.key(seed), 5)
    return {
        "inputs": gaussian(key_list[0], (TOKENS, MODEL_WIDTH), 1.0, 6.0, ((0, 64), (1, 16))),
        "first_factor": gaussian(key_list[1], (IN_BLK, BLOCKS, OUT_BLK), IN_BLK ** -0.5, 0.375, ((1, 16),)),
        "second_factor": gaussian(key_list[2], (OUT_BLK, BLOCKS, OUT_BLK), OUT_BLK ** -0.5, 0.1875, ((1, 16),)),
        "cotangent": gaussian(key_list[3], (HIDDEN_SIZE, TOKENS), 1.0, 6.0, ((0, 16), (1, 64))),
    }


def gelu_backward(pre_act, upstream):
    value, pullback = jax.vjp(lambda v: jax.nn.gelu(v, approximate=True), pre_act)
    return pullback(upstream)[0]

def rounded_activation(value):
    return lax.optimization_barrier(value.astype(jnp.bfloat16)).astype(jnp.float32)

def reference(inputs, first_factor, second_factor, cotangent):
    initial_expanded = first_factor.astype(jnp.float32)
    second_wide = second_factor.astype(jnp.float32)

    def tile_step(carry, tile):
        leading_gradient = carry
        inputs_tile, cot_tile = tile
        row_count = inputs_tile.shape[0]
        block_grouped = inputs_tile.reshape(row_count, BLOCKS, IN_BLK).astype(jnp.float32)
        initial_output = rounded_activation(jnp.einsum('rvh,hva->rva', block_grouped, initial_expanded))
        mixed = initial_output.reshape(row_count, BLOCKS, BLOCKS, GROUP).transpose(0, 2, 1, 3).reshape(row_count, BLOCKS, OUT_BLK)
        pre_act = jnp.einsum('tjm,mjn->jnt', mixed, second_wide)
        upstream = cot_tile.reshape(BLOCKS, OUT_BLK, row_count).astype(jnp.float32)
        pre_grad = rounded_activation(gelu_backward(pre_act, upstream))
        mixed_grad = rounded_activation(jnp.einsum('jnt,mjn->tjm', pre_grad, second_wide))
        output_gradient = mixed_grad.reshape(row_count, BLOCKS, BLOCKS, GROUP).transpose(0, 2, 1, 3).reshape(row_count, BLOCKS, OUT_BLK)
        leading_gradient = leading_gradient + jnp.einsum('cvq,cvs->qvs', block_grouped, output_gradient)
        input_slab = jnp.einsum('ius,yus->iuy', output_gradient, initial_expanded).reshape(row_count, MODEL_WIDTH).astype(jnp.bfloat16)
        return (leading_gradient, input_slab)
    start_one = jnp.zeros((IN_BLK, BLOCKS, OUT_BLK), jnp.float32)
    tiles_in = inputs.reshape(N_DP, TOK_DEV, MODEL_WIDTH)
    tiles_cot = cotangent.reshape(HIDDEN_SIZE, N_DP, TOK_DEV).transpose(1, 0, 2)
    leading_gradient, input_tiles = lax.scan(tile_step, start_one, (tiles_in, tiles_cot))
    factor = jnp.float32(TOKENS ** (-0.5))
    return (input_tiles.reshape(TOKENS, MODEL_WIDTH), leading_gradient * factor)
```

```python
import functools

import jax
import jax.numpy as jnp
from jax import lax
from jax.experimental import pallas as pl
from jax.experimental.pallas import tpu as pltpu
from jax.sharding import PartitionSpec as P

MESH = pl.DeviceIdType.MESH
BF16, F32 = jnp.bfloat16, jnp.float32

Z_HI, CORES, Z_LO = 4, 2, 2


def gelu_slope(v):
    root = 0.7978845608028654
    square = v * v
    t = jnp.tanh(root * (v + 0.044715 * (square * v)))
    return 0.5 * (1.0 + t) + (0.5 * v) * (1.0 - t * t) * (root * (1.0 + 3.0 * 0.044715 * square))


def dot(a, b, contract=((1,), (0,))):
    return lax.dot_general(a, b, (contract, ((), ())), preferred_element_type=F32)


def kernel(
    dims, scale,
    x_hbm, f_hbm, s_hbm, cot_hbm,
    ig_ref, fg_ref,
    x_ref, f_ref, s_ref, cot_ref, st_ref, xpt_ref, pg_ref,
    out_buf, mix_buf, grad_buf, ret_buf,
    term_buf, core_land, x_send, x_land, z_send, z_land,
    load_sem, out_ssem, out_rsem, ret_ssem, ret_rsem,
    core_ssem, core_rsem, x_ssem, x_rsem, z_ssem, z_rsem,
):
    nx, nz, ny, chunks, groups = dims
    per = ny // groups
    nt = ny * Z_LO
    tokens, width = x_ref.shape
    hidden = f_ref.shape[1]
    span = hidden // nt
    pair = span * Z_LO
    tc = tokens // chunks
    rows = width // (nx * nz * CORES)

    dp, tp = lax.axis_index("dp"), lax.axis_index("tensor")
    x = dp // (nz * CORES)
    z = lax.rem(dp // CORES, nz)
    core = lax.rem(dp, CORES)
    y, zl = tp // Z_LO, lax.rem(tp, Z_LO)

    def dp_of(xi, zi, ci):
        return (xi * nz + zi) * CORES + ci

    def shift(s):
        return ny // 2 + (1 - 2 * lax.rem(s, 2)) * ((s + 1) // 2)

    def y_to(s):
        return lax.rem(y + shift(s), ny)

    def y_from(s):
        return lax.rem(y + ny - shift(s), ny)

    loads = [
        pltpu.make_async_copy(src, dst, load_sem.at[i])
        for i, (src, dst) in enumerate(
            ((x_hbm, x_ref), (f_hbm, f_ref), (s_hbm, s_ref), (cot_hbm, cot_ref))
        )
    ]
    for load in loads:
        load.start()

    barrier = pltpu.get_barrier_semaphore()

    def greet(i, _):
        to = lax.rem(tp + i, nt)
        pl.semaphore_signal(barrier, inc=1, device_id=(dp, to), device_id_type=MESH)
        return 0

    lax.fori_loop(1, nt, greet, 0)

    def greet_x(i, _):
        to = dp_of(lax.rem(x + i, nx), z, core)
        pl.semaphore_signal(barrier, inc=1, device_id=(to, tp), device_id_type=MESH)
        return 0

    lax.fori_loop(1, nx, greet_x, 0)

    def greet_z(i, _):
        to = dp_of(x, lax.rem(z + i, nz), core)
        pl.semaphore_signal(barrier, inc=1, device_id=(to, tp), device_id_type=MESH)
        return 0

    lax.fori_loop(1, nz, greet_z, 0)
    sibling = dp_of(x, z, 1 - core)
    pl.semaphore_signal(barrier, inc=1, device_id=(sibling, tp), device_id_type=MESH)

    def exchange(src, dst, ssem, rsem, c, s, dz):
        to = y_to(s) * Z_LO + lax.rem(zl + dz, Z_LO)
        i = s * Z_LO + dz
        return pltpu.make_async_remote_copy(
            src.at[c, to], dst.at[c, tp], ssem.at[c, i], rsem.at[c, i],
            device_id=(dp, to), device_id_type=MESH,
        )

    def landed(dst, ssem, rsem, c, s, dz):
        here = y_from(s) * Z_LO + lax.rem(zl + dz, Z_LO)
        i = s * Z_LO + dz
        pltpu.make_async_remote_copy(
            dst.at[c, here], dst.at[c, here], ssem.at[c, i], rsem.at[c, i],
            device_id=(dp, tp), device_id_type=MESH,
        ).wait_recv()

    def send_out(c, s, dz):
        exchange(out_buf, mix_buf, out_ssem, out_rsem, c, s, dz).start()

    def send_ret(c, s, dz):
        exchange(grad_buf, ret_buf, ret_ssem, ret_rsem, c, s, dz).start()

    loads[0].wait()
    loads[1].wait()

    def first(s):
        to = y_to(s)
        block = f_ref[:, pl.ds(pl.multiple_of(to * pair, pair), pair)]
        made = dot(block, x_ref[...], ((0,), (1,))).astype(BF16)
        for c in range(chunks):
            out_buf[c, pl.ds(to * Z_LO, Z_LO)] = made[:, c * tc : (c + 1) * tc].reshape(Z_LO, span, tc)

    first(0)
    pl.semaphore_wait(barrier, (nt - 1) + (nx - 1) + (nz - 1) + 1)
    for dz in range(Z_LO):
        send_out(0, 0, dz)

    def first_step(s, _):
        first(s)
        for dz in range(Z_LO):
            send_out(0, s, dz)
        return 0

    lax.fori_loop(1, ny - 1, first_step, 0)
    first(ny - 1)
    send_out(0, ny - 1, 1)
    for c in range(chunks):
        mix_buf[c, tp] = out_buf[c, tp]
    for c in range(1, chunks):

        def rest(s, _):
            for dz in range(Z_LO):
                send_out(c, s, dz)
            return 0

        lax.fori_loop(0, ny - 1, rest, 0)
        send_out(c, ny - 1, 1)

    row = lax.broadcasted_iota(jnp.int32, (width, width), 0)
    col = lax.broadcasted_iota(jnp.int32, (width, width), 1)
    half = width // CORES
    r_in = row & (rows - 1)
    z_in = (row & (rows * nz - 1)) - r_in
    x_in = (row & (half - 1)) - z_in - r_in
    c_in = jnp.where(row >= half, rows, 0)
    pick = jnp.where(x_in * CORES + z_in * CORES + c_in + r_in == col, 1.0, 0.0).astype(BF16)
    xpt_ref[...] = dot(pick, x_ref[...], ((1,), (1,))).astype(BF16)
    loads[2].wait()
    tile = min(256, hidden)
    for i in range(hidden // tile):
        st_ref[:, i * tile : (i + 1) * tile] = s_ref[i * tile : (i + 1) * tile, :].T
    loads[3].wait()

    for c in range(chunks):

        def arrive(s, _):
            for dz in range(Z_LO):
                landed(mix_buf, out_ssem, out_rsem, c, s, dz)
            return 0

        lax.fori_loop(0, ny - 1, arrive, 0)
        landed(mix_buf, out_ssem, out_rsem, c, ny - 1, 1)

        def forward(i, _):
            at = pl.ds(pl.multiple_of(i * tile, tile), tile)
            mixed = mix_buf[c].reshape(hidden, tc)
            v = dot(st_ref[at, :], mixed)
            up = cot_ref[at, c * tc : (c + 1) * tc].astype(F32)
            pg_ref[at, :] = (up * gelu_slope(v)).astype(BF16)
            return 0

        lax.fori_loop(0, hidden // tile, forward, 0)

        def back(s):
            to = y_to(s)
            block = s_ref[pl.ds(pl.multiple_of(to * pair, pair), pair), :]
            made = dot(block, pg_ref[...]).astype(BF16)
            grad_buf[c, pl.ds(to * Z_LO, Z_LO)] = made.reshape(Z_LO, span, tc)

        def back_step(s, _):
            back(s)
            for dz in range(Z_LO):
                send_ret(c, s, dz)
            return 0

        lax.fori_loop(0, ny - 1, back_step, 0)
        back(ny - 1)
        send_ret(c, ny - 1, 1)
        ret_buf[c, tp] = grad_buf[c, tp]

    def to_core(g):
        return pltpu.make_async_remote_copy(
            term_buf.at[g, 1 - core], core_land.at[g], core_ssem.at[g], core_rsem.at[g],
            device_id=(sibling, tp), device_id_type=MESH,
        )

    def to_x(g, i):
        other = lax.rem(x + i, nx)
        return pltpu.make_async_remote_copy(
            x_send.at[g, other], x_land.at[g, i], x_ssem.at[g, i], x_rsem.at[g, i],
            device_id=(dp_of(other, z, core), tp), device_id_type=MESH,
        )

    def to_z(g, i):
        other = lax.rem(z + i, nz)
        return pltpu.make_async_remote_copy(
            z_send.at[g, other], z_land.at[g, i], z_ssem.at[g, i], z_rsem.at[g, i],
            device_id=(dp_of(x, other, core), tp), device_id_type=MESH,
        )

    def stage_a(g):
        for p in range(per):
            s = g * per + p
            for c in range(chunks):
                for dz in range(Z_LO):
                    if s < ny - 1 or dz:
                        landed(ret_buf, ret_ssem, ret_rsem, c, s, dz)
            at = pl.ds(y_from(s) * Z_LO, Z_LO)
            term = jnp.zeros((width, pair), F32)
            for c in range(chunks):
                term += dot(
                    xpt_ref[:, c * tc : (c + 1) * tc], ret_buf[c, at].reshape(pair, tc), ((1,), (1,))
                )
            term_buf[g, 0, p] = term[:half]
            term_buf[g, 1, p] = term[half:]
        to_core(g).start()

    def stage_b(g):
        to_core(g).wait_recv()
        for p in range(per):
            total = term_buf[g, core, p] + core_land[g, p]
            core_land[g, p] = total
            x_send[g, :, p] = total.astype(BF16).reshape(nx, half // nx, pair)

        def go(i, _):
            to_x(g, i).start()
            return 0

        lax.fori_loop(1, nx, go, 0)

    def stage_c(g):
        part = half // nx

        def arrive(i, _):
            to_x(g, i).wait_recv()
            return 0

        lax.fori_loop(1, nx, arrive, 0)
        total = core_land[g, :, pl.ds(pl.multiple_of(x * part, part), part)]
        for i in range(1, nx):
            total += x_land[g, i].astype(F32)
        for i in range(nz):
            z_send[g, i] = total[:, i * rows : (i + 1) * rows]

        def go(i, _):
            to_z(g, i).start()
            return 0

        lax.fori_loop(1, nz, go, 0)

    def stage_d(g):
        def arrive(i, _):
            to_z(g, i).wait_recv()
            return 0

        lax.fori_loop(1, nz, arrive, 0)
        total = z_send[g, z]
        for i in range(1, nz):
            total += z_land[g, i]
        for p in range(per):
            at = pl.ds(pl.multiple_of(y_from(g * per + p) * pair, pair), pair)
            fg_ref[:, at] = total[p] * scale

    def input_grad():
        for c in range(chunks):
            made = dot(f_ref[...], ret_buf[c].reshape(hidden, tc))
            ig_ref[c * tc : (c + 1) * tc, :] = made.T.astype(BF16)

    for i in range(groups + 3):
        if i < groups:
            stage_a(i)
        if i == groups - 1:
            input_grad()
        if 0 <= i - 1 < groups:
            stage_b(i - 1)
        if 0 <= i - 2 < groups:
            stage_c(i - 2)
        if 0 <= i - 3 < groups:
            stage_d(i - 3)

    for c in range(chunks):

        def gone(s, _):
            for dz in range(Z_LO):
                exchange(out_buf, mix_buf, out_ssem, out_rsem, c, s, dz).wait_send()
                exchange(grad_buf, ret_buf, ret_ssem, ret_rsem, c, s, dz).wait_send()
            return 0

        lax.fori_loop(0, ny - 1, gone, 0)
        exchange(out_buf, mix_buf, out_ssem, out_rsem, c, ny - 1, 1).wait_send()
        exchange(grad_buf, ret_buf, ret_ssem, ret_rsem, c, ny - 1, 1).wait_send()
    for g in range(groups):
        to_core(g).wait_send()

        def gone_x(i, _):
            to_x(g, i).wait_send()
            return 0

        lax.fori_loop(1, nx, gone_x, 0)

        def gone_z(i, _):
            to_z(g, i).wait_send()
            return 0

        lax.fori_loop(1, nz, gone_z, 0)


def body(n_dp, n_tensor, z_hi, inputs, first_factor, second_factor, cotangent):
    tokens, width = inputs.shape
    hidden = first_factor.shape[2]
    nz, ny = z_hi, n_tensor // Z_LO
    nx = n_dp // (nz * CORES)
    chunks, groups = 2, min(4, ny)
    per = ny // groups
    tc = tokens // chunks
    span = hidden // n_tensor
    pair = span * Z_LO
    half = width // CORES
    part = half // nx
    rows = part // nz
    dma = pltpu.SemaphoreType.DMA
    flow = pltpu.VMEM((chunks, n_tensor, span, tc), BF16)
    input_grad, first_grad = pl.pallas_call(
        functools.partial(kernel, (nx, nz, ny, chunks, groups), (tokens * n_dp) ** (-0.5)),
        out_shape=(
            jax.ShapeDtypeStruct((tokens, width), BF16),
            jax.ShapeDtypeStruct((rows, hidden), F32),
        ),
        in_specs=[pl.BlockSpec(memory_space=pl.ANY)] * 4,
        out_specs=[pl.BlockSpec(memory_space=pltpu.VMEM)] * 2,
        scratch_shapes=[
            pltpu.VMEM((tokens, width), BF16),
            pltpu.VMEM((width, hidden), BF16),
            pltpu.VMEM((hidden, hidden), BF16),
            pltpu.VMEM((hidden, tokens), BF16),
            pltpu.VMEM((hidden, hidden), BF16),
            pltpu.VMEM((width, tokens), BF16),
            pltpu.VMEM((hidden, tc), BF16),
            flow, flow, flow, flow,
            pltpu.VMEM((groups, CORES, per, half, pair), F32),
            pltpu.VMEM((groups, per, half, pair), F32),
            pltpu.VMEM((groups, nx, per, part, pair), BF16),
            pltpu.VMEM((groups, nx, per, part, pair), BF16),
            pltpu.VMEM((groups, nz, per, rows, pair), F32),
            pltpu.VMEM((groups, nz, per, rows, pair), F32),
            dma((4,)),
            dma((chunks, n_tensor)), dma((chunks, n_tensor)),
            dma((chunks, n_tensor)), dma((chunks, n_tensor)),
            dma((groups,)), dma((groups,)),
            dma((groups, nx)), dma((groups, nx)),
            dma((groups, nz)), dma((groups, nz)),
        ],
        compiler_params=pltpu.CompilerParams(
            collective_id=0, has_side_effects=True, vmem_limit_bytes=40 * 2**20
        ),
        cost_estimate=pl.CostEstimate(
            flops=2 * tokens * hidden * (2 * hidden + 3 * width),
            bytes_accessed=2 * hidden * (hidden + 2 * width + tokens),
            transcendentals=hidden * tokens,
        ),
    )(inputs, first_factor.reshape(width, hidden), second_factor.reshape(hidden, hidden), cotangent)
    return input_grad, first_grad.reshape(rows, 1, hidden)


def solution(mesh, z_hi=Z_HI):
    return jax.shard_map(
        functools.partial(body, mesh.shape["dp"], mesh.shape["tensor"], z_hi),
        mesh=mesh,
        in_specs=(
            P("dp", "tensor"),
            P(None, "tensor", None),
            P(None, "tensor", None),
            P("tensor", "dp"),
        ),
        out_specs=(P("dp", "tensor"), P("dp", "tensor", None)),
        check_vma=False,
    )
```

```python
import functools

import jax
import jax.numpy as jnp
from jax import lax
from jax.experimental import pallas as pl
from jax.experimental.pallas import tpu as pltpu
from jax.sharding import PartitionSpec as P

MESH = pl.DeviceIdType.MESH
BF16, F32 = jnp.bfloat16, jnp.float32

Z_HI, CORES, Z_LO = 4, 2, 2


def gelu_slope(v):
    root = 0.7978845608028654
    square = v * v
    t = jnp.tanh(root * (v + 0.044715 * (square * v)))
    return 0.5 * (1.0 + t) + (0.5 * v) * (1.0 - t * t) * (root * (1.0 + 3.0 * 0.044715 * square))


def dot(a, b, contract=((1,), (0,))):
    return lax.dot_general(a, b, (contract, ((), ())), preferred_element_type=F32)


def kernel(
    dims, scale,
    x_hbm, f_hbm, s_hbm, cot_hbm,
    ig_ref, fg_ref,
    x_ref, f_ref, s_ref, cot_ref, st_ref, xpt_ref, pg_ref,
    out_buf, mix_buf, grad_buf, ret_buf,
    term_buf, core_land, xz_send_1, zx_send_1, xz_land_1, zx_land_1, xz_send_2, zx_send_2, xz_land_2, zx_land_2,
    load_sem, out_ssem, out_rsem, ret_ssem, ret_rsem,
    core_ssem, core_rsem, xz_ssem_1, zx_ssem_1, xz_rsem_1, zx_rsem_1, xz_ssem_2, zx_ssem_2, xz_rsem_2, zx_rsem_2,
):
    nx, nz, ny, chunks, groups = dims
    per = ny // groups
    nt = ny * Z_LO
    tokens, width = x_ref.shape
    hidden = f_ref.shape[1]
    span = hidden // nt
    pair = span * Z_LO
    tc = tokens // chunks
    rows = width // (nx * nz * CORES)

    dp, tp = lax.axis_index("dp"), lax.axis_index("tensor")
    x = dp // (nz * CORES)
    z = lax.rem(dp // CORES, nz)
    core = lax.rem(dp, CORES)
    y, zl = tp // Z_LO, lax.rem(tp, Z_LO)

    def dp_of(xi, zi, ci):
        return (xi * nz + zi) * CORES + ci

    def shift(s):
        return ny // 2 + (1 - 2 * lax.rem(s, 2)) * ((s + 1) // 2)

    def y_to(s):
        return lax.rem(y + shift(s), ny)

    def y_from(s):
        return lax.rem(y + ny - shift(s), ny)

    loads = [
        pltpu.make_async_copy(src, dst, load_sem.at[i])
        for i, (src, dst) in enumerate(
            ((x_hbm, x_ref), (f_hbm, f_ref), (s_hbm, s_ref), (cot_hbm, cot_ref))
        )
    ]
    for load in loads:
        load.start()

    barrier = pltpu.get_barrier_semaphore()

    def greet(i, _):
        to = lax.rem(tp + i, nt)
        pl.semaphore_signal(barrier, inc=1, device_id=(dp, to), device_id_type=MESH)
        return 0

    lax.fori_loop(1, nt, greet, 0)

    def greet_x(i, _):
        to = dp_of(lax.rem(x + i, nx), z, core)
        pl.semaphore_signal(barrier, inc=1, device_id=(to, tp), device_id_type=MESH)
        return 0

    lax.fori_loop(1, nx, greet_x, 0)

    def greet_z(i, _):
        to = dp_of(x, lax.rem(z + i, nz), core)
        pl.semaphore_signal(barrier, inc=1, device_id=(to, tp), device_id_type=MESH)
        return 0

    lax.fori_loop(1, nz, greet_z, 0)
    sibling = dp_of(x, z, 1 - core)
    pl.semaphore_signal(barrier, inc=1, device_id=(sibling, tp), device_id_type=MESH)

    def exchange(src, dst, ssem, rsem, c, s, dz):
        to = y_to(s) * Z_LO + lax.rem(zl + dz, Z_LO)
        i = s * Z_LO + dz
        return pltpu.make_async_remote_copy(
            src.at[c, to], dst.at[c, tp], ssem.at[c, i], rsem.at[c, i],
            device_id=(dp, to), device_id_type=MESH,
        )

    def landed(dst, ssem, rsem, c, s, dz):
        here = y_from(s) * Z_LO + lax.rem(zl + dz, Z_LO)
        i = s * Z_LO + dz
        pltpu.make_async_remote_copy(
            dst.at[c, here], dst.at[c, here], ssem.at[c, i], rsem.at[c, i],
            device_id=(dp, tp), device_id_type=MESH,
        ).wait_recv()

    def send_out(c, s, dz):
        exchange(out_buf, mix_buf, out_ssem, out_rsem, c, s, dz).start()

    def send_ret(c, s, dz):
        exchange(grad_buf, ret_buf, ret_ssem, ret_rsem, c, s, dz).start()

    loads[0].wait()
    loads[1].wait()

    def first(s):
        to = y_to(s)
        block = f_ref[:, pl.ds(pl.multiple_of(to * pair, pair), pair)]
        made = dot(block, x_ref[...], ((0,), (1,))).astype(BF16)
        for c in range(chunks):
            out_buf[c, pl.ds(to * Z_LO, Z_LO)] = made[:, c * tc : (c + 1) * tc].reshape(Z_LO, span, tc)

    first(0)
    pl.semaphore_wait(barrier, (nt - 1) + (nx - 1) + (nz - 1) + 1)
    for dz in range(Z_LO):
        send_out(0, 0, dz)

    def first_step(s, _):
        first(s)
        for dz in range(Z_LO):
            send_out(0, s, dz)
        return 0

    lax.fori_loop(1, ny - 1, first_step, 0)
    first(ny - 1)
    send_out(0, ny - 1, 1)
    for c in range(chunks):
        mix_buf[c, tp] = out_buf[c, tp]
    for c in range(1, chunks):

        def rest(s, _):
            for dz in range(Z_LO):
                send_out(c, s, dz)
            return 0

        lax.fori_loop(0, ny - 1, rest, 0)
        send_out(c, ny - 1, 1)

    row = lax.broadcasted_iota(jnp.int32, (width, width), 0)
    col = lax.broadcasted_iota(jnp.int32, (width, width), 1)
    half = width // CORES
    from_core = jnp.where(row >= half, rows, 0)
    r_at = row & (rows - 1)
    unit = row >> (rows.bit_length() - 1)
    for kind in range(2):
        if kind:
            z_at, x_at = (unit >> (nx.bit_length() - 1)) & (nz - 1), unit & (nx - 1)
        else:
            x_at, z_at = (unit >> (nz.bit_length() - 1)) & (nx - 1), unit & (nz - 1)
        taken = (x_at * nz + z_at) * (CORES * rows) + from_core + r_at
        pick = jnp.where(taken == col, 1.0, 0.0).astype(BF16)
        xpt_ref[kind] = dot(pick, x_ref[...], ((1,), (1,))).astype(BF16)
    loads[2].wait()
    tile = min(256, hidden)
    for i in range(hidden // tile):
        st_ref[:, i * tile : (i + 1) * tile] = s_ref[i * tile : (i + 1) * tile, :].T
    loads[3].wait()

    for c in range(chunks):

        def arrive(s, _):
            for dz in range(Z_LO):
                landed(mix_buf, out_ssem, out_rsem, c, s, dz)
            return 0

        lax.fori_loop(0, ny - 1, arrive, 0)
        landed(mix_buf, out_ssem, out_rsem, c, ny - 1, 1)

        def forward(i, _):
            at = pl.ds(pl.multiple_of(i * tile, tile), tile)
            mixed = mix_buf[c].reshape(hidden, tc)
            v = dot(st_ref[at, :], mixed)
            up = cot_ref[at, c * tc : (c + 1) * tc].astype(F32)
            pg_ref[at, :] = (up * gelu_slope(v)).astype(BF16)
            return 0

        lax.fori_loop(0, hidden // tile, forward, 0)

        def back(s):
            to = y_to(s)
            block = s_ref[pl.ds(pl.multiple_of(to * pair, pair), pair), :]
            made = dot(block, pg_ref[...]).astype(BF16)
            grad_buf[c, pl.ds(to * Z_LO, Z_LO)] = made.reshape(Z_LO, span, tc)

        def back_step(s, _):
            back(s)
            for dz in range(Z_LO):
                send_ret(c, s, dz)
            return 0

        lax.fori_loop(0, ny - 1, back_step, 0)
        back(ny - 1)
        send_ret(c, ny - 1, 1)
        ret_buf[c, tp] = grad_buf[c, tp]

    lane = per // 2
    place, count = (x, z), (nx, nz)
    send_1, land_1, ssem_1, rsem_1 = (
        (xz_send_1, zx_send_1), (xz_land_1, zx_land_1), (xz_ssem_1, zx_ssem_1), (xz_rsem_1, zx_rsem_1)
    )
    send_2, land_2, ssem_2, rsem_2 = (
        (xz_send_2, zx_send_2), (xz_land_2, zx_land_2), (xz_ssem_2, zx_ssem_2), (xz_rsem_2, zx_rsem_2)
    )

    def to_core(g):
        return pltpu.make_async_remote_copy(
            term_buf.at[g, 1 - core], core_land.at[g], core_ssem.at[g], core_rsem.at[g],
            device_id=(sibling, tp), device_id_type=MESH,
        )

    def to_first(kind, g, i):
        other = lax.rem(place[kind] + i, count[kind])
        to = dp_of(x, other, core) if kind else dp_of(other, z, core)
        return pltpu.make_async_remote_copy(
            send_1[kind].at[g, other], land_1[kind].at[g, i], ssem_1[kind].at[g, i], rsem_1[kind].at[g, i],
            device_id=(to, tp), device_id_type=MESH,
        )

    def to_second(kind, g, i):
        other = lax.rem(place[1 - kind] + i, count[1 - kind])
        to = dp_of(other, z, core) if kind else dp_of(x, other, core)
        return pltpu.make_async_remote_copy(
            send_2[kind].at[g, other], land_2[kind].at[g, i], ssem_2[kind].at[g, i], rsem_2[kind].at[g, i],
            device_id=(to, tp), device_id_type=MESH,
        )

    def each(n, act):
        def go(i, _):
            act(i)
            return 0

        lax.fori_loop(1, n, go, 0)

    def stage_a(g):
        for p in range(per):
            s = g * per + p
            kind = p // lane
            for c in range(chunks):
                for dz in range(Z_LO):
                    if s < ny - 1 or dz:
                        landed(ret_buf, ret_ssem, ret_rsem, c, s, dz)
            at = pl.ds(y_from(s) * Z_LO, Z_LO)
            term = jnp.zeros((width, pair), F32)
            for c in range(chunks):
                term += dot(
                    xpt_ref[kind, :, c * tc : (c + 1) * tc], ret_buf[c, at].reshape(pair, tc), ((1,), (1,))
                )
            term_buf[g, 0, p] = term[:half]
            term_buf[g, 1, p] = term[half:]
        to_core(g).start()

    def stage_b(g):
        to_core(g).wait_recv()
        for kind in range(2):
            n = count[kind]
            for q in range(lane):
                p = kind * lane + q
                total = term_buf[g, core, p] + core_land[g, p]
                core_land[g, p] = total
                send_1[kind][g, :, q] = total.astype(BF16).reshape(n, half // n, pair)
            each(n, lambda i: to_first(kind, g, i).start())

    def stage_c(g):
        for kind in range(2):
            n = count[kind]
            part = half // n
            each(n, lambda i: to_first(kind, g, i).wait_recv())
            mine = pl.ds(pl.multiple_of(place[kind] * part, part), part)
            total = core_land[g, kind * lane : (kind + 1) * lane, mine]
            for i in range(1, n):
                total += land_1[kind][g, i].astype(F32)
            for i in range(count[1 - kind]):
                send_2[kind][g, i] = total[:, i * rows : (i + 1) * rows]
            each(count[1 - kind], lambda i: to_second(kind, g, i).start())

    def stage_d(g):
        for kind in range(2):
            n = count[1 - kind]
            each(n, lambda i: to_second(kind, g, i).wait_recv())
            total = send_2[kind][g, place[1 - kind]]
            for i in range(1, n):
                total += land_2[kind][g, i]
            for q in range(lane):
                s = g * per + kind * lane + q
                at = pl.ds(pl.multiple_of(y_from(s) * pair, pair), pair)
                fg_ref[:, at] = total[q] * scale

    def input_grad():
        for c in range(chunks):
            made = dot(f_ref[...], ret_buf[c].reshape(hidden, tc))
            ig_ref[c * tc : (c + 1) * tc, :] = made.T.astype(BF16)

    for g in range(groups):
        stage_a(g)
        if g:
            stage_b(g - 1)
    stage_b(groups - 1)
    input_grad()
    for g in range(groups):
        stage_c(g)
    for g in range(groups):
        stage_d(g)

    for c in range(chunks):

        def gone(s, _):
            for dz in range(Z_LO):
                exchange(out_buf, mix_buf, out_ssem, out_rsem, c, s, dz).wait_send()
                exchange(grad_buf, ret_buf, ret_ssem, ret_rsem, c, s, dz).wait_send()
            return 0

        lax.fori_loop(0, ny - 1, gone, 0)
        exchange(out_buf, mix_buf, out_ssem, out_rsem, c, ny - 1, 1).wait_send()
        exchange(grad_buf, ret_buf, ret_ssem, ret_rsem, c, ny - 1, 1).wait_send()
    for g in range(groups):
        to_core(g).wait_send()
        for kind in range(2):
            each(count[kind], lambda i: to_first(kind, g, i).wait_send())
            each(count[1 - kind], lambda i: to_second(kind, g, i).wait_send())


def body(n_dp, n_tensor, z_hi, inputs, first_factor, second_factor, cotangent):
    tokens, width = inputs.shape
    hidden = first_factor.shape[2]
    nz, ny = z_hi, n_tensor // Z_LO
    nx = n_dp // (nz * CORES)
    chunks, groups = 2, min(2, ny // 2)
    per = ny // groups
    tc = tokens // chunks
    span = hidden // n_tensor
    pair = span * Z_LO
    half = width // CORES
    rows = half // (nx * nz)
    firsts = [pltpu.VMEM((groups, n, per // 2, half // n, pair), BF16) for n in (nx, nz)]
    seconds = [pltpu.VMEM((groups, n, per // 2, rows, pair), F32) for n in (nz, nx)]
    dma = pltpu.SemaphoreType.DMA
    flow = pltpu.VMEM((chunks, n_tensor, span, tc), BF16)
    input_grad, first_grad = pl.pallas_call(
        functools.partial(kernel, (nx, nz, ny, chunks, groups), (tokens * n_dp) ** (-0.5)),
        out_shape=(
            jax.ShapeDtypeStruct((tokens, width), BF16),
            jax.ShapeDtypeStruct((rows, hidden), F32),
        ),
        in_specs=[pl.BlockSpec(memory_space=pl.ANY)] * 4,
        out_specs=[pl.BlockSpec(memory_space=pltpu.VMEM)] * 2,
        scratch_shapes=[
            pltpu.VMEM((tokens, width), BF16),
            pltpu.VMEM((width, hidden), BF16),
            pltpu.VMEM((hidden, hidden), BF16),
            pltpu.VMEM((hidden, tokens), BF16),
            pltpu.VMEM((hidden, hidden), BF16),
            pltpu.VMEM((2, width, tokens), BF16),
            pltpu.VMEM((hidden, tc), BF16),
            flow, flow, flow, flow,
            pltpu.VMEM((groups, CORES, per, half, pair), F32),
            pltpu.VMEM((groups, per, half, pair), F32),
            *firsts, *firsts, *seconds, *seconds,
            dma((4,)),
            dma((chunks, n_tensor)), dma((chunks, n_tensor)),
            dma((chunks, n_tensor)), dma((chunks, n_tensor)),
            dma((groups,)), dma((groups,)),
            dma((groups, nx)), dma((groups, nz)), dma((groups, nx)), dma((groups, nz)),
            dma((groups, nz)), dma((groups, nx)), dma((groups, nz)), dma((groups, nx)),
        ],
        compiler_params=pltpu.CompilerParams(
            collective_id=0, has_side_effects=True, vmem_limit_bytes=60 * 2**20
        ),
        cost_estimate=pl.CostEstimate(
            flops=2 * tokens * hidden * (2 * hidden + 3 * width),
            bytes_accessed=2 * hidden * (hidden + 2 * width + tokens),
            transcendentals=hidden * tokens,
        ),
    )(inputs, first_factor.reshape(width, hidden), second_factor.reshape(hidden, hidden), cotangent)
    return input_grad, first_grad.reshape(rows, 1, hidden)


def solution(mesh, z_hi=Z_HI):
    return jax.shard_map(
        functools.partial(body, mesh.shape["dp"], mesh.shape["tensor"], z_hi),
        mesh=mesh,
        in_specs=(
            P("dp", "tensor"),
            P(None, "tensor", None),
            P(None, "tensor", None),
            P("tensor", "dp"),
        ),
        out_specs=(P("dp", "tensor"), P("dp", "tensor", None)),
        check_vma=False,
    )
```

```python
import functools

import jax
import jax.numpy as jnp
from jax import lax
from jax.experimental import pallas as pl
from jax.experimental.pallas import tpu as pltpu
from jax.sharding import PartitionSpec as P

MESH = pl.DeviceIdType.MESH
BF16, F32 = jnp.bfloat16, jnp.float32

Z_HI, CORES, Z_LO = 4, 2, 2


def gelu_slope(v):
    root = 0.7978845608028654
    square = v * v
    t = jnp.tanh(root * (v + 0.044715 * (square * v)))
    return 0.5 * (1.0 + t) + (0.5 * v) * (1.0 - t * t) * (root * (1.0 + 3.0 * 0.044715 * square))


def dot(a, b, contract=((1,), (0,))):
    return lax.dot_general(a, b, (contract, ((), ())), preferred_element_type=F32)


def kernel(
    dims, scale,
    x_hbm, f_hbm, s_hbm, cot_hbm,
    ig_ref, fg_ref,
    x_ref, f_ref, s_ref, cot_ref, st_ref, xpt_ref, pg_ref,
    out_buf, mix_buf, grad_buf, ret_buf,
    term_buf, core_land, xz_send_1, zx_send_1, xz_land_1, zx_land_1, xz_send_2, zx_send_2, xz_land_2, zx_land_2,
    load_sem, out_ssem, out_rsem, ret_ssem, ret_rsem,
    core_ssem, core_rsem, xz_ssem_1, zx_ssem_1, xz_rsem_1, zx_rsem_1, xz_ssem_2, zx_ssem_2, xz_rsem_2, zx_rsem_2,
):
    nx, nz, ny, chunks, groups = dims
    per = ny // groups
    nt = ny * Z_LO
    tokens, width = x_ref.shape
    hidden = f_ref.shape[1]
    span = hidden // nt
    pair = span * Z_LO
    tc = tokens // chunks
    rows = width // (nx * nz * CORES)

    dp, tp = lax.axis_index("dp"), lax.axis_index("tensor")
    x = dp // (nz * CORES)
    z = lax.rem(dp // CORES, nz)
    core = lax.rem(dp, CORES)
    y, zl = tp // Z_LO, lax.rem(tp, Z_LO)

    def dp_of(xi, zi, ci):
        return (xi * nz + zi) * CORES + ci

    def shift(s):
        k = ny // 2 - 1 - s // 2
        odd = lax.rem(s, 2)
        return k + odd * (ny - 2 * k) + (s // (ny - 2)) * (1 - odd) * (ny // 2)

    def y_to(s):
        return lax.rem(y + shift(s), ny)

    def y_from(s):
        return lax.rem(y + ny - shift(s), ny)

    loads = [
        pltpu.make_async_copy(src, dst, load_sem.at[i])
        for i, (src, dst) in enumerate(
            ((x_hbm, x_ref), (f_hbm, f_ref), (s_hbm, s_ref), (cot_hbm, cot_ref))
        )
    ]
    for load in loads:
        load.start()

    barrier = pltpu.get_barrier_semaphore()

    def greet(i, _):
        to = lax.rem(tp + i, nt)
        pl.semaphore_signal(barrier, inc=1, device_id=(dp, to), device_id_type=MESH)
        return 0

    lax.fori_loop(1, nt, greet, 0)

    def greet_x(i, _):
        to = dp_of(lax.rem(x + i, nx), z, core)
        pl.semaphore_signal(barrier, inc=1, device_id=(to, tp), device_id_type=MESH)
        return 0

    lax.fori_loop(1, nx, greet_x, 0)

    def greet_z(i, _):
        to = dp_of(x, lax.rem(z + i, nz), core)
        pl.semaphore_signal(barrier, inc=1, device_id=(to, tp), device_id_type=MESH)
        return 0

    lax.fori_loop(1, nz, greet_z, 0)
    sibling = dp_of(x, z, 1 - core)
    pl.semaphore_signal(barrier, inc=1, device_id=(sibling, tp), device_id_type=MESH)

    def taken(buf, index, sem):
        return pltpu.make_async_copy(buf.at[index], buf.at[index], sem)

    def exchange(src, dst, ssem, rsem, c, s, dz):
        to = y_to(s) * Z_LO + lax.rem(zl + dz, Z_LO)
        return pltpu.make_async_remote_copy(
            src.at[c, to], dst.at[c, tp], ssem, rsem, device_id=(dp, to), device_id_type=MESH
        )

    def send_out(c, s, dz):
        exchange(out_buf, mix_buf, out_ssem.at[c], out_rsem.at[c], c, s, dz).start()

    def send_ret(c, g, s, dz):
        exchange(grad_buf, ret_buf, ret_ssem.at[c], ret_rsem.at[c, g], c, s, dz).start()

    loads[0].wait()
    loads[1].wait()

    def first(s):
        to = y_to(s)
        block = f_ref[:, pl.ds(pl.multiple_of(to * pair, pair), pair)]
        made = dot(block, x_ref[...], ((0,), (1,))).astype(BF16)
        for c in range(chunks):
            out_buf[c, pl.ds(to * Z_LO, Z_LO)] = made[:, c * tc : (c + 1) * tc].reshape(Z_LO, span, tc)

    def send_all(send, c, start, stop):
        def far(s, _):
            send(c, s, 1)
            return 0

        def near(s, _):
            send(c, s, 0)
            return 0

        lax.fori_loop(start, stop, far, 0)
        lax.fori_loop(start, min(stop, ny - 1), near, 0)

    first(0)
    pl.semaphore_wait(barrier, (nt - 1) + (nx - 1) + (nz - 1) + 1)
    send_out(0, 0, 1)

    def first_step(s, _):
        first(s)
        send_out(0, s, 1)
        return 0

    def first_near(s, _):
        send_out(0, s, 0)
        return 0

    lax.fori_loop(1, ny, first_step, 0)
    lax.fori_loop(0, ny - 1, first_near, 0)
    for c in range(1, chunks):
        send_all(send_out, c, 0, ny)
    for c in range(chunks):
        mix_buf[c, tp] = out_buf[c, tp]

    row = lax.broadcasted_iota(jnp.int32, (width, width), 0)
    col = lax.broadcasted_iota(jnp.int32, (width, width), 1)
    half = width // CORES
    from_core = jnp.where(row >= half, rows, 0)
    r_at = row & (rows - 1)
    unit = row >> (rows.bit_length() - 1)
    for kind in range(2):
        if kind:
            z_at, x_at = (unit >> (nx.bit_length() - 1)) & (nz - 1), unit & (nx - 1)
        else:
            x_at, z_at = (unit >> (nz.bit_length() - 1)) & (nx - 1), unit & (nz - 1)
        source = (x_at * nz + z_at) * (CORES * rows) + from_core + r_at
        pick = jnp.where(source == col, 1.0, 0.0).astype(BF16)
        xpt_ref[kind] = dot(pick, x_ref[...], ((1,), (1,))).astype(BF16)
    loads[2].wait()
    tile = min(256, hidden)
    for i in range(hidden // tile):
        st_ref[:, i * tile : (i + 1) * tile] = s_ref[i * tile : (i + 1) * tile, :].T
    loads[3].wait()

    for c in range(chunks):

        taken(mix_buf, (c, pl.ds(0, nt - 1)), out_rsem.at[c]).wait()

        def forward(i, _):
            at = pl.ds(pl.multiple_of(i * tile, tile), tile)
            mixed = mix_buf[c].reshape(hidden, tc)
            v = dot(st_ref[at, :], mixed)
            up = cot_ref[at, c * tc : (c + 1) * tc].astype(F32)
            pg_ref[at, :] = (up * gelu_slope(v)).astype(BF16)
            return 0

        lax.fori_loop(0, hidden // tile, forward, 0)

        def back(i):
            ends = [y_to(2 * i + j) for j in range(2)]
            block = jnp.concatenate(
                [s_ref[pl.ds(pl.multiple_of(to * pair, pair), pair), :] for to in ends], axis=0
            )
            made = dot(block, pg_ref[...]).astype(BF16).reshape(2, Z_LO, span, tc)
            for j in range(2):
                grad_buf[c, pl.ds(ends[j] * Z_LO, Z_LO)] = made[j]

        for g in range(groups):

            def back_step(i, _):
                back(i)
                for j in range(2):
                    send_ret(c, g, 2 * i + j, 1)
                return 0

            def back_near(s, _):
                send_ret(c, g, s, 0)
                return 0

            lax.fori_loop(g * per // 2, (g + 1) * per // 2, back_step, 0)
            lax.fori_loop(g * per, min((g + 1) * per, ny - 1), back_near, 0)
        ret_buf[c, tp] = grad_buf[c, tp]

    lane = per // 2
    place, count = (x, z), (nx, nz)
    send_1, land_1, ssem_1, rsem_1 = (
        (xz_send_1, zx_send_1), (xz_land_1, zx_land_1), (xz_ssem_1, zx_ssem_1), (xz_rsem_1, zx_rsem_1)
    )
    send_2, land_2, ssem_2, rsem_2 = (
        (xz_send_2, zx_send_2), (xz_land_2, zx_land_2), (xz_ssem_2, zx_ssem_2), (xz_rsem_2, zx_rsem_2)
    )

    def to_core(g):
        return pltpu.make_async_remote_copy(
            term_buf.at[g, 1 - core], core_land.at[g], core_ssem.at[g], core_rsem.at[g],
            device_id=(sibling, tp), device_id_type=MESH,
        )

    def to_first(kind, g, i):
        other = lax.rem(place[kind] + i, count[kind])
        to = dp_of(x, other, core) if kind else dp_of(other, z, core)
        return pltpu.make_async_remote_copy(
            send_1[kind].at[g, other], land_1[kind].at[g, i], ssem_1[kind].at[g], rsem_1[kind].at[g],
            device_id=(to, tp), device_id_type=MESH,
        )

    def to_second(kind, g, i):
        other = lax.rem(place[1 - kind] + i, count[1 - kind])
        to = dp_of(other, z, core) if kind else dp_of(x, other, core)
        return pltpu.make_async_remote_copy(
            send_2[kind].at[g, other], land_2[kind].at[g, i], ssem_2[kind].at[g], rsem_2[kind].at[g],
            device_id=(to, tp), device_id_type=MESH,
        )

    def each(n, act):
        def go(i, _):
            act(i)
            return 0

        lax.fori_loop(1, n, go, 0)

    def stage_a(g):
        came = per * Z_LO - (g == groups - 1)
        for c in range(chunks):
            taken(ret_buf, (c, pl.ds(0, came)), ret_rsem.at[c, g]).wait()
        for p in range(per):
            s = g * per + p
            kind = p // lane
            at = pl.ds(y_from(s) * Z_LO, Z_LO)
            term = jnp.zeros((width, pair), F32)
            for c in range(chunks):
                term += dot(
                    xpt_ref[kind, :, c * tc : (c + 1) * tc], ret_buf[c, at].reshape(pair, tc), ((1,), (1,))
                )
            term_buf[g, 0, p] = term[:half]
            term_buf[g, 1, p] = term[half:]
        to_core(g).start()

    def stage_b(g):
        to_core(g).wait_recv()
        for kind in range(2):
            n = count[kind]
            for q in range(lane):
                p = kind * lane + q
                total = term_buf[g, core, p] + core_land[g, p]
                core_land[g, p] = total
                send_1[kind][g, :, q] = total.astype(BF16).reshape(n, half // n, pair)
            each(n, lambda i: to_first(kind, g, i).start())

    def stage_c(g):
        for kind in range(2):
            n = count[kind]
            part = half // n
            taken(land_1[kind], (g, pl.ds(1, n - 1)), rsem_1[kind].at[g]).wait()
            mine = pl.ds(pl.multiple_of(place[kind] * part, part), part)
            total = core_land[g, kind * lane : (kind + 1) * lane, mine]
            for i in range(1, n):
                total += land_1[kind][g, i].astype(F32)
            for i in range(count[1 - kind]):
                send_2[kind][g, i] = total[:, i * rows : (i + 1) * rows]
            each(count[1 - kind], lambda i: to_second(kind, g, i).start())

    def stage_d(g):
        for kind in range(2):
            n = count[1 - kind]
            taken(land_2[kind], (g, pl.ds(1, n - 1)), rsem_2[kind].at[g]).wait()
            total = send_2[kind][g, place[1 - kind]]
            for i in range(1, n):
                total += land_2[kind][g, i]
            for q in range(lane):
                s = g * per + kind * lane + q
                at = pl.ds(pl.multiple_of(y_from(s) * pair, pair), pair)
                fg_ref[:, at] = total[q] * scale

    def input_grad():
        for c in range(chunks):
            made = dot(f_ref[...], ret_buf[c].reshape(hidden, tc))
            ig_ref[c * tc : (c + 1) * tc, :] = made.T.astype(BF16)

    for g in range(groups):
        stage_a(g)
        if g:
            stage_b(g - 1)
    stage_b(groups - 1)
    input_grad()
    for c in range(chunks):
        taken(out_buf, (c, pl.ds(0, nt - 1)), out_ssem.at[c]).wait()
        taken(grad_buf, (c, pl.ds(0, nt - 1)), ret_ssem.at[c]).wait()
    for g in range(groups):
        to_core(g).wait_send()
    for g in range(groups):
        stage_c(g)
    for g in range(groups):
        for kind in range(2):
            taken(send_1[kind], (g, pl.ds(1, count[kind] - 1)), ssem_1[kind].at[g]).wait()
    for g in range(groups):
        stage_d(g)
    for g in range(groups):
        for kind in range(2):
            taken(send_2[kind], (g, pl.ds(1, count[1 - kind] - 1)), ssem_2[kind].at[g]).wait()


def body(n_dp, n_tensor, z_hi, inputs, first_factor, second_factor, cotangent):
    tokens, width = inputs.shape
    hidden = first_factor.shape[2]
    nz, ny = z_hi, n_tensor // Z_LO
    nx = n_dp // (nz * CORES)
    chunks, groups = 2, min(4, ny // 2)
    per = ny // groups
    tc = tokens // chunks
    span = hidden // n_tensor
    pair = span * Z_LO
    half = width // CORES
    rows = half // (nx * nz)
    firsts = [pltpu.VMEM((groups, n, per // 2, half // n, pair), BF16) for n in (nx, nz)]
    seconds = [pltpu.VMEM((groups, n, per // 2, rows, pair), F32) for n in (nz, nx)]
    dma = pltpu.SemaphoreType.DMA
    flow = pltpu.VMEM((chunks, n_tensor, span, tc), BF16)
    input_grad, first_grad = pl.pallas_call(
        functools.partial(kernel, (nx, nz, ny, chunks, groups), (tokens * n_dp) ** (-0.5)),
        out_shape=(
            jax.ShapeDtypeStruct((tokens, width), BF16),
            jax.ShapeDtypeStruct((rows, hidden), F32),
        ),
        in_specs=[pl.BlockSpec(memory_space=pl.ANY)] * 4,
        out_specs=[pl.BlockSpec(memory_space=pltpu.VMEM)] * 2,
        scratch_shapes=[
            pltpu.VMEM((tokens, width), BF16),
            pltpu.VMEM((width, hidden), BF16),
            pltpu.VMEM((hidden, hidden), BF16),
            pltpu.VMEM((hidden, tokens), BF16),
            pltpu.VMEM((hidden, hidden), BF16),
            pltpu.VMEM((2, width, tokens), BF16),
            pltpu.VMEM((hidden, tc), BF16),
            flow, flow, flow, flow,
            pltpu.VMEM((groups, CORES, per, half, pair), F32),
            pltpu.VMEM((groups, per, half, pair), F32),
            *firsts, *firsts, *seconds, *seconds,
            dma((4,)),
            dma((chunks,)), dma((chunks,)), dma((chunks,)), dma((chunks, groups)),
            *[dma((groups,))] * 10,
        ],
        compiler_params=pltpu.CompilerParams(
            collective_id=0, has_side_effects=True, vmem_limit_bytes=60 * 2**20
        ),
        cost_estimate=pl.CostEstimate(
            flops=2 * tokens * hidden * (2 * hidden + 3 * width),
            bytes_accessed=2 * hidden * (hidden + 2 * width + tokens),
            transcendentals=hidden * tokens,
        ),
    )(inputs, first_factor.reshape(width, hidden), second_factor.reshape(hidden, hidden), cotangent)
    return input_grad, first_grad.reshape(rows, 1, hidden)


def solution(mesh, z_hi=Z_HI):
    return jax.shard_map(
        functools.partial(body, mesh.shape["dp"], mesh.shape["tensor"], z_hi),
        mesh=mesh,
        in_specs=(
            P("dp", "tensor"),
            P(None, "tensor", None),
            P(None, "tensor", None),
            P("tensor", "dp"),
        ),
        out_specs=(P("dp", "tensor"), P("dp", "tensor", None)),
        check_vma=False,
    )
```

```python
import functools

import jax
import jax.numpy as jnp
from jax import lax
from jax.experimental import pallas as pl
from jax.experimental.pallas import tpu as pltpu
from jax.sharding import PartitionSpec as P

MESH = pl.DeviceIdType.MESH
BF16, F32 = jnp.bfloat16, jnp.float32

Z_HI, CORES, Z_LO = 4, 2, 2


def gelu_slope(v):
    root = 0.7978845608028654
    square = v * v
    t = jnp.tanh(root * (v + 0.044715 * (square * v)))
    return 0.5 * (1.0 + t) + (0.5 * v) * (1.0 - t * t) * (root * (1.0 + 3.0 * 0.044715 * square))


def dot(a, b, contract=((1,), (0,))):
    return lax.dot_general(a, b, (contract, ((), ())), preferred_element_type=F32)


def kernel(
    dims, scale,
    x_hbm, f_hbm, s_hbm, cot_hbm,
    ig_ref, fg_ref,
    x_ref, f_ref, s_ref, cot_ref, st_ref, xpt_ref, pg_ref,
    out_buf, mix_buf, grad_buf, ret_buf,
    term_buf, core_land, xz_send_1, zx_send_1, xz_land_1, zx_land_1, xz_send_2, zx_send_2, xz_land_2, zx_land_2,
    load_sem, out_ssem, out_rsem, ret_ssem, ret_rsem,
    core_ssem, core_rsem, xz_ssem_1, zx_ssem_1, xz_rsem_1, zx_rsem_1, xz_ssem_2, zx_ssem_2, xz_rsem_2, zx_rsem_2,
):
    nx, nz, ny, chunks, groups = dims
    per = ny // groups
    nt = ny * Z_LO
    tokens, width = x_ref.shape
    hidden = f_ref.shape[1]
    span = hidden // nt
    pair = span * Z_LO
    tc = tokens // chunks
    rows = width // (nx * nz * CORES)

    dp, tp = lax.axis_index("dp"), lax.axis_index("tensor")
    x = dp // (nz * CORES)
    z = lax.rem(dp // CORES, nz)
    core = lax.rem(dp, CORES)
    y, zl = tp // Z_LO, lax.rem(tp, Z_LO)

    def dp_of(xi, zi, ci):
        return (xi * nz + zi) * CORES + ci

    def shift(s):
        k = ny // 2 - 1 - s // 2
        odd = lax.rem(s, 2)
        return k + odd * (ny - 2 * k) + (s // (ny - 2)) * (1 - odd) * (ny // 2)

    def y_to(s):
        return lax.rem(y + shift(s), ny)

    def y_from(s):
        return lax.rem(y + ny - shift(s), ny)

    loads = [
        pltpu.make_async_copy(src, dst, load_sem.at[i])
        for i, (src, dst) in enumerate(
            ((x_hbm, x_ref), (f_hbm, f_ref), (s_hbm, s_ref), (cot_hbm, cot_ref))
        )
    ]
    for load in loads:
        load.start()

    barrier = pltpu.get_barrier_semaphore()

    def greet(i, _):
        to = lax.rem(tp + i, nt)
        pl.semaphore_signal(barrier, inc=1, device_id=(dp, to), device_id_type=MESH)
        return 0

    lax.fori_loop(1, nt, greet, 0)

    def greet_x(i, _):
        to = dp_of(lax.rem(x + i, nx), z, core)
        pl.semaphore_signal(barrier, inc=1, device_id=(to, tp), device_id_type=MESH)
        return 0

    lax.fori_loop(1, nx, greet_x, 0)

    def greet_z(i, _):
        to = dp_of(x, lax.rem(z + i, nz), core)
        pl.semaphore_signal(barrier, inc=1, device_id=(to, tp), device_id_type=MESH)
        return 0

    lax.fori_loop(1, nz, greet_z, 0)
    sibling = dp_of(x, z, 1 - core)
    pl.semaphore_signal(barrier, inc=1, device_id=(sibling, tp), device_id_type=MESH)

    def taken(buf, index, sem):
        return pltpu.make_async_copy(buf.at[index], buf.at[index], sem)

    def exchange(src, dst, ssem, rsem, c, s, dz):
        to = y_to(s) * Z_LO + lax.rem(zl + dz, Z_LO)
        return pltpu.make_async_remote_copy(
            src.at[c, to], dst.at[c, tp], ssem, rsem, device_id=(dp, to), device_id_type=MESH
        )

    def send_out(c, s, dz):
        exchange(out_buf, mix_buf, out_ssem.at[c], out_rsem.at[c], c, s, dz).start()

    def send_ret(c, g, s, dz):
        exchange(grad_buf, ret_buf, ret_ssem.at[c], ret_rsem.at[c, g], c, s, dz).start()

    loads[0].wait()
    loads[1].wait()

    def first(s):
        to = y_to(s)
        block = f_ref[:, pl.ds(pl.multiple_of(to * pair, pair), pair)]
        made = dot(block, x_ref[...], ((0,), (1,))).astype(BF16)
        for c in range(chunks):
            out_buf[c, pl.ds(to * Z_LO, Z_LO)] = made[:, c * tc : (c + 1) * tc].reshape(Z_LO, span, tc)

    def send_all(send, c, start, stop):
        def far(s, _):
            send(c, s, 1)
            return 0

        def near(s, _):
            send(c, s, 0)
            return 0

        lax.fori_loop(start, stop, far, 0)
        lax.fori_loop(start, min(stop, ny - 1), near, 0)

    first(0)
    pl.semaphore_wait(barrier, (nt - 1) + (nx - 1) + (nz - 1) + 1)
    send_out(0, 0, 1)

    def first_step(s, _):
        first(s)
        send_out(0, s, 1)
        return 0

    def first_near(s, _):
        send_out(0, s, 0)
        return 0

    lax.fori_loop(1, ny, first_step, 0)
    lax.fori_loop(0, ny - 1, first_near, 0)
    for c in range(1, chunks):
        send_all(send_out, c, 0, ny)
    for c in range(chunks):
        mix_buf[c, tp] = out_buf[c, tp]

    row = lax.broadcasted_iota(jnp.int32, (width, width), 0)
    col = lax.broadcasted_iota(jnp.int32, (width, width), 1)
    half = width // CORES
    from_core = jnp.where(row >= half, rows, 0)
    r_at = row & (rows - 1)
    unit = row >> (rows.bit_length() - 1)
    for kind in range(2):
        if kind:
            z_at, x_at = (unit >> (nx.bit_length() - 1)) & (nz - 1), unit & (nx - 1)
        else:
            x_at, z_at = (unit >> (nz.bit_length() - 1)) & (nx - 1), unit & (nz - 1)
        source = (x_at * nz + z_at) * (CORES * rows) + from_core + r_at
        pick = jnp.where(source == col, 1.0, 0.0).astype(BF16)
        xpt_ref[kind] = dot(pick, x_ref[...], ((1,), (1,))).astype(BF16)
    loads[2].wait()
    tile = min(256, hidden)
    for i in range(hidden // tile):
        st_ref[:, i * tile : (i + 1) * tile] = s_ref[i * tile : (i + 1) * tile, :].T
    loads[3].wait()

    for c in range(chunks):

        taken(mix_buf, (c, pl.ds(0, nt - 1)), out_rsem.at[c]).wait()

        def forward(i, _):
            at = pl.ds(pl.multiple_of(i * tile, tile), tile)
            mixed = mix_buf[c].reshape(hidden, tc)
            v = dot(st_ref[at, :], mixed)
            up = cot_ref[at, c * tc : (c + 1) * tc].astype(F32)
            pg_ref[at, :] = (up * gelu_slope(v)).astype(BF16)
            return 0

        lax.fori_loop(0, hidden // tile, forward, 0)

        def back(i):
            ends = [y_to(2 * i + j) for j in range(2)]
            block = jnp.concatenate(
                [s_ref[pl.ds(pl.multiple_of(to * pair, pair), pair), :] for to in ends], axis=0
            )
            made = dot(block, pg_ref[...]).astype(BF16).reshape(2, Z_LO, span, tc)
            for j in range(2):
                grad_buf[c, pl.ds(ends[j] * Z_LO, Z_LO)] = made[j]

        for g in range(groups):

            def back_step(i, _):
                back(i)
                for j in range(2):
                    send_ret(c, g, 2 * i + j, 1)
                return 0

            def back_near(s, _):
                send_ret(c, g, s, 0)
                return 0

            lax.fori_loop(g * per // 2, (g + 1) * per // 2, back_step, 0)
            lax.fori_loop(g * per, min((g + 1) * per, ny - 1), back_near, 0)
        ret_buf[c, tp] = grad_buf[c, tp]

    lane = per // 2
    place, count = (x, z), (nx, nz)
    send_1, land_1, ssem_1, rsem_1 = (
        (xz_send_1, zx_send_1), (xz_land_1, zx_land_1), (xz_ssem_1, zx_ssem_1), (xz_rsem_1, zx_rsem_1)
    )
    send_2, land_2, ssem_2, rsem_2 = (
        (xz_send_2, zx_send_2), (xz_land_2, zx_land_2), (xz_ssem_2, zx_ssem_2), (xz_rsem_2, zx_rsem_2)
    )

    def to_core(g):
        return pltpu.make_async_remote_copy(
            term_buf.at[g, 1 - core], core_land.at[g], core_ssem.at[g], core_rsem.at[g],
            device_id=(sibling, tp), device_id_type=MESH,
        )

    def to_first(kind, g, i):
        other = lax.rem(place[kind] + i, count[kind])
        to = dp_of(x, other, core) if kind else dp_of(other, z, core)
        return pltpu.make_async_remote_copy(
            send_1[kind].at[g, other], land_1[kind].at[g, i], ssem_1[kind].at[g], rsem_1[kind].at[g],
            device_id=(to, tp), device_id_type=MESH,
        )

    def to_second(kind, g, i):
        other = lax.rem(place[1 - kind] + i, count[1 - kind])
        to = dp_of(other, z, core) if kind else dp_of(x, other, core)
        return pltpu.make_async_remote_copy(
            send_2[kind].at[g, other], land_2[kind].at[g, i], ssem_2[kind].at[g], rsem_2[kind].at[g],
            device_id=(to, tp), device_id_type=MESH,
        )

    def each(n, act):
        def go(i, _):
            act(i)
            return 0

        lax.fori_loop(1, n, go, 0)

    def stage_a(g):
        came = per * Z_LO - (g == groups - 1)
        for c in range(chunks):
            taken(ret_buf, (c, pl.ds(0, came)), ret_rsem.at[c, g]).wait()
        for p in range(per):
            s = g * per + p
            kind = p // lane
            at = pl.ds(y_from(s) * Z_LO, Z_LO)
            term = jnp.zeros((width, pair), F32)
            for c in range(chunks):
                term += dot(
                    xpt_ref[kind, :, c * tc : (c + 1) * tc], ret_buf[c, at].reshape(pair, tc), ((1,), (1,))
                )
            term_buf[g, 0, p] = term[:half]
            term_buf[g, 1, p] = term[half:]
        to_core(g).start()

    def stage_b(g):
        to_core(g).wait_recv()
        for kind in range(2):
            n = count[kind]
            for q in range(lane):
                p = kind * lane + q
                total = term_buf[g, core, p] + core_land[g, p]
                core_land[g, p] = total
                send_1[kind][g, :, q] = total.astype(BF16).reshape(n, half // n, pair)
            each(n, lambda i: to_first(kind, g, i).start())

    def stage_c(g):
        for kind in range(2):
            n = count[kind]
            part = half // n
            taken(land_1[kind], (g, pl.ds(1, n - 1)), rsem_1[kind].at[g]).wait()
            mine = pl.ds(pl.multiple_of(place[kind] * part, part), part)
            total = core_land[g, kind * lane : (kind + 1) * lane, mine]
            for i in range(1, n):
                total += land_1[kind][g, i].astype(F32)
            for i in range(count[1 - kind]):
                send_2[kind][g, i] = total[:, i * rows : (i + 1) * rows]
            each(count[1 - kind], lambda i: to_second(kind, g, i).start())

    def stage_d(g):
        for kind in range(2):
            n = count[1 - kind]
            taken(land_2[kind], (g, pl.ds(1, n - 1)), rsem_2[kind].at[g]).wait()
            total = send_2[kind][g, place[1 - kind]]
            for i in range(1, n):
                total += land_2[kind][g, i]
            for q in range(lane):
                s = g * per + kind * lane + q
                at = pl.ds(pl.multiple_of(y_from(s) * pair, pair), pair)
                fg_ref[:, at] = total[q] * scale

    def input_grad():
        for c in range(chunks):
            made = dot(f_ref[...], ret_buf[c].reshape(hidden, tc))
            ig_ref[c * tc : (c + 1) * tc, :] = made.T.astype(BF16)

    for g in range(groups):
        stage_a(g)
        if g:
            stage_b(g - 1)
    stage_b(groups - 1)
    input_grad()
    for c in range(chunks):
        taken(out_buf, (c, pl.ds(0, nt - 1)), out_ssem.at[c]).wait()
        taken(grad_buf, (c, pl.ds(0, nt - 1)), ret_ssem.at[c]).wait()
    for g in range(groups):
        to_core(g).wait_send()
    for g in range(groups):
        stage_c(g)
    for g in range(groups):
        for kind in range(2):
            taken(send_1[kind], (g, pl.ds(1, count[kind] - 1)), ssem_1[kind].at[g]).wait()
    for g in range(groups):
        stage_d(g)
    for g in range(groups):
        for kind in range(2):
            taken(send_2[kind], (g, pl.ds(1, count[1 - kind] - 1)), ssem_2[kind].at[g]).wait()


def body(n_dp, n_tensor, z_hi, inputs, first_factor, second_factor, cotangent):
    tokens, width = inputs.shape
    hidden = first_factor.shape[2]
    nz, ny = z_hi, n_tensor // Z_LO
    nx = n_dp // (nz * CORES)
    chunks, groups = 2, min(4, ny // 2)
    per = ny // groups
    tc = tokens // chunks
    span = hidden // n_tensor
    pair = span * Z_LO
    half = width // CORES
    rows = half // (nx * nz)
    firsts = [pltpu.VMEM((groups, n, per // 2, half // n, pair), BF16) for n in (nx, nz)]
    seconds = [pltpu.VMEM((groups, n, per // 2, rows, pair), F32) for n in (nz, nx)]
    dma = pltpu.SemaphoreType.DMA
    flow = pltpu.VMEM((chunks, n_tensor, span, tc), BF16)
    input_grad, first_grad = pl.pallas_call(
        functools.partial(kernel, (nx, nz, ny, chunks, groups), (tokens * n_dp) ** (-0.5)),
        out_shape=(
            jax.ShapeDtypeStruct((tokens, width), BF16),
            jax.ShapeDtypeStruct((rows, hidden), F32),
        ),
        in_specs=[pl.BlockSpec(memory_space=pl.ANY)] * 4,
        out_specs=[pl.BlockSpec(memory_space=pltpu.VMEM)] * 2,
        scratch_shapes=[
            pltpu.VMEM((tokens, width), BF16),
            pltpu.VMEM((width, hidden), BF16),
            pltpu.VMEM((hidden, hidden), BF16),
            pltpu.VMEM((hidden, tokens), BF16),
            pltpu.VMEM((hidden, hidden), BF16),
            pltpu.VMEM((2, width, tokens), BF16),
            pltpu.VMEM((hidden, tc), BF16),
            flow, flow, flow, flow,
            pltpu.VMEM((groups, CORES, per, half, pair), F32),
            pltpu.VMEM((groups, per, half, pair), F32),
            *firsts, *firsts, *seconds, *seconds,
            dma((4,)),
            dma((chunks,)), dma((chunks,)), dma((chunks,)), dma((chunks, groups)),
            *[dma((groups,))] * 10,
        ],
        compiler_params=pltpu.CompilerParams(
            collective_id=0, has_side_effects=True, vmem_limit_bytes=55040 * 2**10
        ),
        cost_estimate=pl.CostEstimate(
            flops=2 * tokens * hidden * (2 * hidden + 3 * width),
            bytes_accessed=2 * hidden * (hidden + 2 * width + tokens),
            transcendentals=hidden * tokens,
        ),
    )(inputs, first_factor.reshape(width, hidden), second_factor.reshape(hidden, hidden), cotangent)
    return input_grad, first_grad.reshape(rows, 1, hidden)


def solution(mesh, z_hi=Z_HI):
    return jax.shard_map(
        functools.partial(body, mesh.shape["dp"], mesh.shape["tensor"], z_hi),
        mesh=mesh,
        in_specs=(
            P("dp", "tensor"),
            P(None, "tensor", None),
            P(None, "tensor", None),
            P("tensor", "dp"),
        ),
        out_specs=(P("dp", "tensor"), P("dp", "tensor", None)),
        check_vma=False,
    )
```

```python
import functools

import jax
import jax.numpy as jnp
from jax import lax
from jax.experimental import pallas as pl
from jax.experimental.pallas import tpu as pltpu
from jax.sharding import PartitionSpec as P

MESH = pl.DeviceIdType.MESH
BF16, F32 = jnp.bfloat16, jnp.float32

Z_HI, CORES, Z_LO = 4, 2, 2


def gelu_slope(v):
    root = 0.7978845608028654
    square = v * v
    t = jnp.tanh(root * (v + 0.044715 * (square * v)))
    return 0.5 * (1.0 + t) + (0.5 * v) * (1.0 - t * t) * (root * (1.0 + 3.0 * 0.044715 * square))


def dot(a, b, contract=((1,), (0,))):
    return lax.dot_general(a, b, (contract, ((), ())), preferred_element_type=F32)


def kernel(
    dims, scale,
    x_hbm, f_hbm, s_hbm, cot_hbm,
    ig_ref, fg_ref,
    x_ref, f_ref, s_ref, cot_ref, st_ref, xpt_ref, pg_ref,
    out_buf, mix_buf, grad_buf, ret_buf,
    term_buf, core_land, xz_send_1, zx_send_1, xz_land_1, zx_land_1, xz_send_2, zx_send_2, xz_land_2, zx_land_2,
    load_sem, out_ssem, out_rsem, ret_ssem, ret_rsem,
    core_ssem, core_rsem, xz_ssem_1, zx_ssem_1, xz_rsem_1, zx_rsem_1, xz_ssem_2, zx_ssem_2, xz_rsem_2, zx_rsem_2,
):
    nx, nz, ny, chunks, groups = dims
    per = ny // groups
    nt = ny * Z_LO
    tokens, width = x_ref.shape
    hidden = f_ref.shape[1]
    span = hidden // nt
    pair = span * Z_LO
    tc = tokens // chunks
    rows = width // (nx * nz * CORES)

    dp, tp = lax.axis_index("dp"), lax.axis_index("tensor")
    x = dp // (nz * CORES)
    z = lax.rem(dp // CORES, nz)
    core = lax.rem(dp, CORES)
    y, zl = tp // Z_LO, lax.rem(tp, Z_LO)

    def dp_of(xi, zi, ci):
        return (xi * nz + zi) * CORES + ci

    def shift(s):
        k = ny // 2 - 1 - s // 2
        odd = lax.rem(s, 2)
        return k + odd * (ny - 2 * k) + (s // (ny - 2)) * (1 - odd) * (ny // 2)

    def y_to(s):
        return lax.rem(y + shift(s), ny)

    def y_from(s):
        return lax.rem(y + ny - shift(s), ny)

    loads = [
        pltpu.make_async_copy(src, dst, load_sem.at[i])
        for i, (src, dst) in enumerate(
            ((x_hbm, x_ref), (f_hbm, f_ref), (s_hbm, s_ref), (cot_hbm, cot_ref))
        )
    ]
    for load in loads:
        load.start()

    barrier = pltpu.get_barrier_semaphore()

    def greet(i, _):
        to = lax.rem(tp + i, nt)
        pl.semaphore_signal(barrier, inc=1, device_id=(dp, to), device_id_type=MESH)
        return 0

    lax.fori_loop(1, nt, greet, 0)

    def greet_x(i, _):
        to = dp_of(lax.rem(x + i, nx), z, core)
        pl.semaphore_signal(barrier, inc=1, device_id=(to, tp), device_id_type=MESH)
        return 0

    lax.fori_loop(1, nx, greet_x, 0)

    def greet_z(i, _):
        to = dp_of(x, lax.rem(z + i, nz), core)
        pl.semaphore_signal(barrier, inc=1, device_id=(to, tp), device_id_type=MESH)
        return 0

    lax.fori_loop(1, nz, greet_z, 0)
    sibling = dp_of(x, z, 1 - core)
    pl.semaphore_signal(barrier, inc=1, device_id=(sibling, tp), device_id_type=MESH)

    def taken(buf, index, sem):
        return pltpu.make_async_copy(buf.at[index], buf.at[index], sem)

    def exchange(src, dst, ssem, rsem, c, s, dz):
        to = y_to(s) * Z_LO + lax.rem(zl + dz, Z_LO)
        return pltpu.make_async_remote_copy(
            src.at[c, to], dst.at[c, tp], ssem, rsem, device_id=(dp, to), device_id_type=MESH
        )

    def send_out(c, s, dz):
        exchange(out_buf, mix_buf, out_ssem.at[c], out_rsem.at[c], c, s, dz).start()

    def send_ret(c, g, s, dz):
        exchange(grad_buf, ret_buf, ret_ssem.at[c], ret_rsem.at[c, g], c, s, dz).start()

    loads[0].wait()
    loads[1].wait()

    def first(s):
        to = y_to(s)
        block = f_ref[:, pl.ds(pl.multiple_of(to * pair, pair), pair)]
        made = dot(block, x_ref[...], ((0,), (1,))).astype(BF16)
        for c in range(chunks):
            out_buf[c, pl.ds(to * Z_LO, Z_LO)] = made[:, c * tc : (c + 1) * tc].reshape(Z_LO, span, tc)

    def send_all(send, c, start, stop):
        def far(s, _):
            send(c, s, 1)
            return 0

        def near(s, _):
            send(c, s, 0)
            return 0

        lax.fori_loop(start, stop, far, 0)
        lax.fori_loop(start, min(stop, ny - 1), near, 0)

    first(0)
    pl.semaphore_wait(barrier, (nt - 1) + (nx - 1) + (nz - 1) + 1)
    send_out(0, 0, 1)

    def first_step(s, _):
        first(s)
        send_out(0, s, 1)
        return 0

    def first_near(s, _):
        send_out(0, s, 0)
        return 0

    lax.fori_loop(1, ny, first_step, 0)
    lax.fori_loop(0, ny - 1, first_near, 0)
    for c in range(1, chunks):
        send_all(send_out, c, 0, ny)
    for c in range(chunks):
        mix_buf[c, tp] = out_buf[c, tp]

    row = lax.broadcasted_iota(jnp.int32, (width, width), 0)
    col = lax.broadcasted_iota(jnp.int32, (width, width), 1)
    half = width // CORES
    from_core = jnp.where(row >= half, rows, 0)
    r_at = row & (rows - 1)
    unit = row >> (rows.bit_length() - 1)
    for kind in range(2):
        if kind:
            z_at, x_at = (unit >> (nx.bit_length() - 1)) & (nz - 1), unit & (nx - 1)
        else:
            x_at, z_at = (unit >> (nz.bit_length() - 1)) & (nx - 1), unit & (nz - 1)
        source = (x_at * nz + z_at) * (CORES * rows) + from_core + r_at
        pick = jnp.where(source == col, 1.0, 0.0).astype(BF16)
        xpt_ref[kind] = dot(pick, x_ref[...], ((1,), (1,))).astype(BF16)
    loads[2].wait()
    tile = min(256, hidden)
    for i in range(hidden // tile):
        st_ref[:, i * tile : (i + 1) * tile] = s_ref[i * tile : (i + 1) * tile, :].T
    loads[3].wait()

    for c in range(chunks):

        taken(mix_buf, (c, pl.ds(0, nt - 1)), out_rsem.at[c]).wait()

        def forward(i, _):
            at = pl.ds(pl.multiple_of(i * tile, tile), tile)
            mixed = mix_buf[c].reshape(hidden, tc)
            v = dot(st_ref[at, :], mixed)
            up = cot_ref[at, c * tc : (c + 1) * tc].astype(F32)
            pg_ref[at, :] = (up * gelu_slope(v)).astype(BF16)
            return 0

        lax.fori_loop(0, hidden // tile, forward, 0)

        def back(i):
            ends = [y_to(2 * i + j) for j in range(2)]
            block = jnp.concatenate(
                [s_ref[pl.ds(pl.multiple_of(to * pair, pair), pair), :] for to in ends], axis=0
            )
            made = dot(block, pg_ref[...]).astype(BF16).reshape(2, Z_LO, span, tc)
            for j in range(2):
                grad_buf[c, pl.ds(ends[j] * Z_LO, Z_LO)] = made[j]

        for g in range(groups):

            def back_step(i, _):
                back(i)
                for j in range(2):
                    send_ret(c, g, 2 * i + j, 1)
                return 0

            def back_near(s, _):
                send_ret(c, g, s, 0)
                return 0

            lax.fori_loop(g * per // 2, (g + 1) * per // 2, back_step, 0)
            lax.fori_loop(g * per, min((g + 1) * per, ny - 1), back_near, 0)
        ret_buf[c, tp] = grad_buf[c, tp]

    place, count = (x, z), (nx, nz)
    send_1, land_1, ssem_1, rsem_1 = (
        (xz_send_1, zx_send_1), (xz_land_1, zx_land_1), (xz_ssem_1, zx_ssem_1), (xz_rsem_1, zx_rsem_1)
    )
    send_2, land_2, ssem_2, rsem_2 = (
        (xz_send_2, zx_send_2), (xz_land_2, zx_land_2), (xz_ssem_2, zx_ssem_2), (xz_rsem_2, zx_rsem_2)
    )

    def to_core(g):
        return pltpu.make_async_remote_copy(
            term_buf.at[g, 1 - core], core_land.at[g], core_ssem.at[g], core_rsem.at[g],
            device_id=(sibling, tp), device_id_type=MESH,
        )

    def to_first(kind, g, i):
        other = lax.rem(place[kind] + i, count[kind])
        to = dp_of(x, other, core) if kind else dp_of(other, z, core)
        return pltpu.make_async_remote_copy(
            send_1[kind].at[g // 2, other], land_1[kind].at[g // 2, i], ssem_1[kind].at[g // 2], rsem_1[kind].at[g // 2],
            device_id=(to, tp), device_id_type=MESH,
        )

    def to_second(kind, g, i):
        other = lax.rem(place[1 - kind] + i, count[1 - kind])
        to = dp_of(other, z, core) if kind else dp_of(x, other, core)
        return pltpu.make_async_remote_copy(
            send_2[kind].at[g // 2, other], land_2[kind].at[g // 2, i], ssem_2[kind].at[g // 2], rsem_2[kind].at[g // 2],
            device_id=(to, tp), device_id_type=MESH,
        )

    def each(n, act):
        for i in range(1, n):
            act(i)

    def stage_a(g):
        came = per * Z_LO - (g == groups - 1)
        for c in range(chunks):
            taken(ret_buf, (c, pl.ds(0, came)), ret_rsem.at[c, g]).wait()
        for p in range(per):
            at = pl.ds(y_from(g * per + p) * Z_LO, Z_LO)
            term = jnp.zeros((width, pair), F32)
            for c in range(chunks):
                term += dot(
                    xpt_ref[g % 2, :, c * tc : (c + 1) * tc], ret_buf[c, at].reshape(pair, tc), ((1,), (1,))
                )
            term_buf[g, 0, p] = term[:half]
            term_buf[g, 1, p] = term[half:]
        to_core(g).start()

    def stage_b(g):
        kind, h = g % 2, g // 2
        n = count[kind]
        to_core(g).wait_recv()
        for p in range(per):
            total = term_buf[g, core, p] + core_land[g, p]
            core_land[g, p] = total
            send_1[kind][h, :, p] = total.astype(BF16).reshape(n, half // n, pair)
        each(n, lambda i: to_first(kind, g, i).start())

    def stage_c(g):
        kind, h = g % 2, g // 2
        n = count[kind]
        part = half // n
        taken(land_1[kind], (h, pl.ds(1, n - 1)), rsem_1[kind].at[h]).wait()
        mine = pl.ds(pl.multiple_of(place[kind] * part, part), part)
        total = core_land[g, :, mine]
        for i in range(1, n):
            total += land_1[kind][h, i].astype(F32)
        for i in range(count[1 - kind]):
            send_2[kind][h, i] = total[:, i * rows : (i + 1) * rows]
        each(count[1 - kind], lambda i: to_second(kind, g, i).start())

    def stage_d(g):
        kind, h = g % 2, g // 2
        n = count[1 - kind]
        taken(land_2[kind], (h, pl.ds(1, n - 1)), rsem_2[kind].at[h]).wait()
        total = send_2[kind][h, place[1 - kind]]
        for i in range(1, n):
            total += land_2[kind][h, i]
        for p in range(per):
            at = pl.ds(pl.multiple_of(y_from(g * per + p) * pair, pair), pair)
            fg_ref[:, at] = total[p] * scale

    def input_grad():
        for c in range(chunks):
            made = dot(f_ref[...], ret_buf[c].reshape(hidden, tc))
            ig_ref[c * tc : (c + 1) * tc, :] = made.T.astype(BF16)

    for g in range(groups):
        stage_a(g)
        if g:
            stage_b(g - 1)
    stage_b(groups - 1)
    input_grad()
    for c in range(chunks):
        taken(out_buf, (c, pl.ds(0, nt - 1)), out_ssem.at[c]).wait()
        taken(grad_buf, (c, pl.ds(0, nt - 1)), ret_ssem.at[c]).wait()
    for g in range(groups):
        to_core(g).wait_send()
    for g in range(groups):
        stage_c(g)
    for g in range(groups):
        kind, h = g % 2, g // 2
        taken(send_1[kind], (h, pl.ds(1, count[kind] - 1)), ssem_1[kind].at[h]).wait()
    for g in range(groups):
        stage_d(g)
    for g in range(groups):
        kind, h = g % 2, g // 2
        taken(send_2[kind], (h, pl.ds(1, count[1 - kind] - 1)), ssem_2[kind].at[h]).wait()


def body(n_dp, n_tensor, z_hi, inputs, first_factor, second_factor, cotangent):
    tokens, width = inputs.shape
    hidden = first_factor.shape[2]
    nz, ny = z_hi, n_tensor // Z_LO
    nx = n_dp // (nz * CORES)
    chunks, groups = 2, min(4, ny // 2)
    per = ny // groups
    tc = tokens // chunks
    span = hidden // n_tensor
    pair = span * Z_LO
    half = width // CORES
    rows = half // (nx * nz)
    firsts = [pltpu.VMEM((groups // 2, n, per, half // n, pair), BF16) for n in (nx, nz)]
    seconds = [pltpu.VMEM((groups // 2, n, per, rows, pair), F32) for n in (nz, nx)]
    dma = pltpu.SemaphoreType.DMA
    flow = pltpu.VMEM((chunks, n_tensor, span, tc), BF16)
    input_grad, first_grad = pl.pallas_call(
        functools.partial(kernel, (nx, nz, ny, chunks, groups), (tokens * n_dp) ** (-0.5)),
        out_shape=(
            jax.ShapeDtypeStruct((tokens, width), BF16),
            jax.ShapeDtypeStruct((rows, hidden), F32),
        ),
        in_specs=[pl.BlockSpec(memory_space=pl.ANY)] * 4,
        out_specs=[pl.BlockSpec(memory_space=pltpu.VMEM)] * 2,
        scratch_shapes=[
            pltpu.VMEM((tokens, width), BF16),
            pltpu.VMEM((width, hidden), BF16),
            pltpu.VMEM((hidden, hidden), BF16),
            pltpu.VMEM((hidden, tokens), BF16),
            pltpu.VMEM((hidden, hidden), BF16),
            pltpu.VMEM((2, width, tokens), BF16),
            pltpu.VMEM((hidden, tc), BF16),
            flow, flow, flow, flow,
            pltpu.VMEM((groups, CORES, per, half, pair), F32),
            pltpu.VMEM((groups, per, half, pair), F32),
            *firsts, *firsts, *seconds, *seconds,
            dma((4,)),
            dma((chunks,)), dma((chunks,)), dma((chunks,)), dma((chunks, groups)),
            dma((groups,)), dma((groups,)), *[dma((groups // 2,))] * 8,
        ],
        compiler_params=pltpu.CompilerParams(
            collective_id=0, has_side_effects=True, vmem_limit_bytes=55040 * 2**10
        ),
        cost_estimate=pl.CostEstimate(
            flops=2 * tokens * hidden * (2 * hidden + 3 * width),
            bytes_accessed=2 * hidden * (hidden + 2 * width + tokens),
            transcendentals=hidden * tokens,
        ),
    )(inputs, first_factor.reshape(width, hidden), second_factor.reshape(hidden, hidden), cotangent)
    return input_grad, first_grad.reshape(rows, 1, hidden)


def solution(mesh, z_hi=Z_HI):
    return jax.shard_map(
        functools.partial(body, mesh.shape["dp"], mesh.shape["tensor"], z_hi),
        mesh=mesh,
        in_specs=(
            P("dp", "tensor"),
            P(None, "tensor", None),
            P(None, "tensor", None),
            P("tensor", "dp"),
        ),
        out_specs=(P("dp", "tensor"), P("dp", "tensor", None)),
        check_vma=False,
    )
```
